32 devices in a mesh: env: 2 (over y), gx: 4 (over x, core), gy: 4 (over z).
Axes of the slice: x: 2, y: 2, z: 4, core: 2. Of those that a mesh axis runs over, the one named last changes fastest.
Arguments:
- old_state: float32 [1024, 3, 128, 128], P(('env', 'gx', 'gy')), parts along dimension 0, may hold values from -0.8 to 1.5, as said below
- bed: float32 [512, 128, 128], P(('env', 'gx', 'gy')), parts along dimension 0, may hold values from -0.5 to 0.5
- roughness: float32 [512, 128, 128], P(('env', 'gx', 'gy')), parts along dimension 0, may hold values from 0.02 to 0.2
- levels: int32 [512], P(('env', 'gx', 'gy')), parts along dimension 0, may hold values from 0 to 2
- sources: int32 [512], P('env'), parts along dimension 0, may hold values from 0 to 511, as said below
- neighbours: int32 [512, 8], P(('env', 'gx', 'gy')), parts along dimension 0, may hold values from -1 to 255, as said below
- face_codes: int32 [512, 4], P(('env', 'gx', 'gy')), parts along dimension 0, may hold values from 0 to 4, as said below
- step_index: int32 [6], P('env'), parts along dimension 0, may hold values from 4 to 6
Outputs:
- new_state: float32 [512, 3, 128, 128], P(('env', 'gx', 'gy')), parts along dimension 0
The draws below stay inside these ranges and needn't reach their ends.
There are 2 independent parts, one for each index of `env`. The reference program is written for one: setup_inputs(seed, part) draws one part's arguments, and reference() takes and returns one part's arrays. A program takes and returns all parts, laid end to end along the dimension named above; each array names one. Nothing has to cross between parts.
Inputs may be any that keep to these rules, and one draw needn't show every extreme that they name: Patch g lies on device g // 16 of gx+gy (gx slowest) and takes old slot sources[g], held by device sources[g] // 32; that device has the same gy index and a gx index that differs by at most one. No old slot is used twice. From one device to the one beside it along gx, in each direction, at most 8 patches move, and exactly 8 for some pair in every draw. `neighbours`: entries 2f and 2f+1 name the patches beside face f, -1 for a wall. A named patch lies on the same device as patch g, or for face 0 on the device one lower along gx, face 1 one higher along gx, face 2 one lower along gy, face 3 one higher along gy. Entry 2f+1 equals entry 2f unless the face code is 3; then it lies on the same device as entry 2f. `face_codes`: 0: the patch beside has the same level; 1: it is coarser and this face meets the lower half of its face; 2: the upper half; 3: two finer patches (entry 2f along the lower half, 2f+1 along the upper); 4: a wall, both entries -1. `old_state`: component 0 lies in 0.5 to 1.5; components 1 and 2 in -0.8 to 0.8.
All inputs are finite; a program needn't handle non-finite values.
Results may differ from the reference program's by a relative error of at most 0.0003.
Values sent between devices are 32-bit elements; how exact they have to be, the bound alone decides.
A program may use at most 128 MiB of HBM per device.

```python
import math
import jax
import jax.numpy as jnp
from jax import lax

PS = 128
P_DEV = 16
STEPS = 3
MOVE = 8
OLD_CAP = 32
PATCHES = 256
OLD_PATCHES = 512
N_GX = 4
N_GY = 4


def layout(key):
    subkeys = jax.random.split(jax.random.fold_in(key, 101), 10)
    devices = N_GX * N_GY
    dev_ids = jnp.arange(devices, dtype=jnp.int32)
    gx_ids = dev_ids // N_GY
    from_left = jax.random.randint(subkeys[0], (devices,), 0, MOVE + 1)
    from_right = jax.random.randint(subkeys[1], (devices,), 0, MOVE + 1)
    from_left = jnp.where(gx_ids == 0, 0, from_left)
    from_right = jnp.where(gx_ids == N_GX - 1, 0, from_right)
    pick_left = jax.random.randint(subkeys[2], (), N_GY, devices)
    pick_right = jax.random.randint(subkeys[3], (), 0, devices - N_GY)
    from_left = from_left.at[pick_left].set(MOVE)
    from_right = from_right.at[pick_right].set(MOVE)
    staying = P_DEV - from_left - from_right
    left_of_next = jnp.concatenate([from_left[N_GY:], jnp.zeros((N_GY,), jnp.int32)])
    old_perms = jax.vmap(lambda sub: jax.random.permutation(sub, OLD_CAP))(jax.random.split(subkeys[4], devices))
    new_perms = jax.vmap(lambda sub: jax.random.permutation(sub, P_DEV))(jax.random.split(subkeys[5], devices))
    position = jnp.arange(P_DEV, dtype=jnp.int32)[None, :]
    is_left = position < from_left[:, None]
    is_right = jnp.logical_and(jnp.logical_not(is_left), position < (from_left + from_right)[:, None])
    rank = jnp.where(is_left, position, jnp.where(is_right, position - from_left[:, None], position - from_left[:, None] - from_right[:, None]))
    owner = dev_ids[:, None]
    source_dev = jnp.where(is_left, owner - N_GY, jnp.where(is_right, owner + N_GY, owner))
    source_dev = jnp.clip(source_dev, 0, devices - 1)
    offset = jnp.where(is_left, staying[source_dev] + rank, jnp.where(is_right, staying[source_dev] + left_of_next[source_dev] + rank, rank))
    old_slot = source_dev * OLD_CAP + jnp.take_along_axis(old_perms[source_dev], offset[:, :, None], axis=2)[:, :, 0]
    sources = jnp.take_along_axis(old_slot, new_perms, axis=1).reshape(-1).astype(jnp.int32)
    level_draw = jax.random.randint(subkeys[6], (PATCHES,), 0, 8)
    levels = jnp.where(level_draw < 1, 0, jnp.where(level_draw < 3, 1, 2)).astype(jnp.int32)
    patch_ids = jnp.arange(PATCHES, dtype=jnp.int32)
    home = patch_ids // P_DEV
    home_x = home // N_GY
    home_y = home % N_GY
    offsets = jnp.array([-N_GY, N_GY, -1, 1], jnp.int32)
    valid = jnp.stack([home_x > 0, home_x < N_GX - 1, home_y > 0, home_y < N_GY - 1], axis=1)
    lottery = jax.random.randint(subkeys[7], (PATCHES, 4), 0, 16)
    is_wall = jnp.logical_or(lottery == 0, jnp.logical_and(jnp.logical_not(valid), lottery < 8))
    remote = jnp.logical_and(valid, lottery >= 2)
    target_dev = jnp.where(remote, home[:, None] + offsets[None, :], home[:, None])
    locals_first = jax.random.randint(subkeys[8], (PATCHES, 4), 0, P_DEV)
    first = target_dev * P_DEV + locals_first
    subs = jax.random.split(subkeys[9], 2)
    halves = jax.random.randint(subs[0], (PATCHES, 4), 0, 2)
    other_local = (locals_first + 1 + jax.random.randint(subs[1], (PATCHES, 4), 0, P_DEV - 1)) % P_DEV
    mine_level = levels[:, None]
    their_level = levels[first]
    codes = jnp.where(their_level == mine_level, 0, jnp.where(their_level < mine_level, 1 + halves, 3))
    codes = jnp.where(is_wall, 4, codes).astype(jnp.int32)
    second = jnp.where(codes == 3, target_dev * P_DEV + other_local, first)
    first = jnp.where(is_wall, -1, first)
    second = jnp.where(is_wall, -1, second)
    neighbours = jnp.stack([first, second], axis=-1).reshape(PATCHES, 8).astype(jnp.int32)
    return (sources, levels, neighbours, codes)


def draw_sources(key, part):
    return layout(key)[0]


def draw_levels(key, part):
    return layout(key)[1]


def draw_neighbours(key, part):
    return layout(key)[2]


def draw_face_codes(key, part):
    return layout(key)[3]


def draw_old_state(key, part):
    key = jax.random.fold_in(key, 3)
    side_key, depth_key, sign_key, flow_key = jax.random.split(key, 4)
    shape = (OLD_PATCHES, PS, PS)
    depth_spread = 0.25
    flow_least = 0.4
    upper_side = jax.random.uniform(side_key, shape, jnp.float32) < 0.5
    depth_offset = depth_spread * jax.random.uniform(depth_key, shape, jnp.float32)
    depth = jnp.where(upper_side, 1.5 - depth_offset, 0.5 + depth_offset)
    flow_sign = jnp.where(jax.random.uniform(sign_key, (2,) + shape, jnp.float32) < 0.5, -1.0, 1.0)
    flow_size = flow_least + (0.8 - flow_least) * jax.random.uniform(flow_key, (2,) + shape, jnp.float32)
    flow = flow_sign * flow_size
    return jnp.concatenate([depth[:, None], jnp.moveaxis(flow, 0, 1)], axis=1).astype(jnp.float32)


def steps_of(stream_key, shape, cuts, least, top_value):
    gain, own = 1.0, jax.random.fold_in(stream_key, 6)
    for dim, blocks in cuts:
        heights = jnp.exp(jax.random.uniform(jax.random.fold_in(own, dim), (blocks,), jnp.float32, least / len(cuts), top_value / len(cuts)))
        gain = gain * jnp.repeat(heights, shape[dim] // blocks).reshape([-1 if axis == dim else 1 for axis in range(len(shape))])
    return gain


def setup_inputs(seed: int = 0, part: int = 0) -> dict:
    seeds = jax.random.split(jax.random.key(seed), 9)
    part_splits = jax.random.split(jax.random.fold_in(seeds[8], part), 9)
    old_state = draw_old_state(jax.random.fold_in(jax.random.fold_in(seeds[8], part), 71), part)
    bed = jnp.clip(jax.random.uniform(part_splits[1], (PATCHES, PS, PS), jnp.float32, -0.5, 0.5) * steps_of(part_splits[1], (PATCHES, PS, PS), ((0, 16),), -0.4, 0.0), -0.5, 0.5)
    roughness = jnp.clip(jnp.exp(math.log(0.2) - 2.3025851 * jax.random.uniform(part_splits[2], (PATCHES, PS, PS), jnp.float32) ** steps_of(part_splits[2], (PATCHES, PS, PS), ((0, 16),), -0.2, 0.2)), 0.02, 0.2)
    levels = draw_levels(jax.random.fold_in(jax.random.fold_in(seeds[8], part), 71), part)
    sources = draw_sources(jax.random.fold_in(jax.random.fold_in(seeds[8], part), 71), part)
    neighbours = draw_neighbours(jax.random.fold_in(jax.random.fold_in(seeds[8], part), 71), part)
    face_codes = draw_face_codes(jax.random.fold_in(jax.random.fold_in(seeds[8], part), 71), part)
    step_index = jax.random.randint(part_splits[7], (STEPS,), 4, 7).astype(jnp.int32)
    return dict(old_state=old_state, bed=bed, roughness=roughness, levels=levels, sources=sources, neighbours=neighbours, face_codes=face_codes, step_index=step_index)


GRAVITY = 9.81
COARSE_SPACING = 32.0
STEP_BASE = 0.15

def minmod(first_diff, second_diff):
    return 0.5 * (jnp.sign(first_diff) + jnp.sign(second_diff)) * jnp.minimum(jnp.abs(first_diff), jnp.abs(second_diff))

def take_range(array, start, stop, axis):
    return lax.slice_in_dim(array, start, stop, axis=axis)

def strips_of(field):
    west = jnp.swapaxes(field[..., 0:4], -1, -2)
    east = jnp.swapaxes(jnp.flip(field[..., -4:], -1), -1, -2)
    south = field[..., 0:4, :]
    north = jnp.flip(field[..., -4:, :], -2)
    return jnp.stack([west, east, south, north], axis=1)

def combine(first, second, own, codes, signs):
    half = first.shape[-1] // 2
    same = first[..., 0:2, :]
    edge = first[..., 0, :]
    lower = jnp.repeat(edge[..., :half], 2, axis=-1)
    upper = jnp.repeat(edge[..., half:], 2, axis=-1)
    lower = jnp.stack([lower, lower], axis=-2)
    upper = jnp.stack([upper, upper], axis=-2)

    def pooled(strips):
        blocks = strips.reshape(strips.shape[:-2] + (2, 2, half, 2))
        return lax.optimization_barrier(jnp.mean(blocks, axis=(-3, -1)))
    finer = jnp.concatenate([pooled(first), pooled(second)], axis=-1)
    mirror = own[..., 0:2, :] * signs[None, :, :, None, None]
    code = codes[:, :, None, None, None]
    return jnp.where(code == 0, same, jnp.where(code == 1, lower, jnp.where(code == 2, upper, jnp.where(code == 3, finer, mirror))))

def pad_field(field, ghosts):
    west = jnp.swapaxes(jnp.flip(ghosts[:, 0], 2), -1, -2)
    east = jnp.swapaxes(ghosts[:, 1], -1, -2)
    south = jnp.flip(ghosts[:, 2], 2)
    north = ghosts[:, 3]
    along_x = jnp.concatenate([west, field, east], axis=-1)
    along_y = jnp.concatenate([south, field, north], axis=-2)
    return (along_x, along_y)

def sweep_axis(depth, normal, tangent, bed_padded, spacing, axis):
    length = depth.shape[axis] - 4

    def faces(values):
        diffs = take_range(values, 1, length + 4, axis) - take_range(values, 0, length + 3, axis)
        slopes = minmod(take_range(diffs, 0, length + 2, axis), take_range(diffs, 1, length + 3, axis))
        left = take_range(values, 1, length + 2, axis) + 0.5 * take_range(slopes, 0, length + 1, axis)
        right = take_range(values, 2, length + 3, axis) - 0.5 * take_range(slopes, 1, length + 2, axis)
        return (left, right)
    depth_left, depth_right = faces(depth)
    normal_left, normal_right = faces(normal)
    tangent_left, tangent_right = faces(tangent)
    speed_left = normal_left / depth_left
    speed_right = normal_right / depth_right
    celerity_left = jnp.sqrt(GRAVITY * depth_left)
    celerity_right = jnp.sqrt(GRAVITY * depth_right)
    slowest = jnp.minimum(jnp.minimum(speed_left - celerity_left, speed_right - celerity_right), 0.0)
    fastest = jnp.maximum(jnp.maximum(speed_left + celerity_left, speed_right + celerity_right), 0.0)

    def hll_flux(flux_left, flux_right, value_left, value_right):
        return (fastest * flux_left - slowest * flux_right + fastest * slowest * (value_right - value_left)) / (fastest - slowest)
    mass_flux = hll_flux(normal_left, normal_right, depth_left, depth_right)
    normal_flux = hll_flux(normal_left * speed_left + 0.5 * GRAVITY * depth_left * depth_left, normal_right * speed_right + 0.5 * GRAVITY * depth_right * depth_right, normal_left, normal_right)
    tangent_flux = hll_flux(tangent_left * speed_left, tangent_right * speed_right, tangent_left, tangent_right)

    def divergence(flux):
        return (take_range(flux, 1, length + 1, axis) - take_range(flux, 0, length, axis)) / spacing
    centre_depth = take_range(depth, 2, length + 2, axis)
    bed_slope = (take_range(bed_padded, 3, length + 3, axis) - take_range(bed_padded, 1, length + 1, axis)) / (2.0 * spacing)
    return (-divergence(mass_flux), -divergence(normal_flux) - GRAVITY * centre_depth * bed_slope, -divergence(tangent_flux))

def tendency(field, ghosts, bed_x, bed_y, roughness, spacing):
    along_x, along_y = pad_field(field, ghosts)
    mass_x, east_x, north_x = sweep_axis(along_x[:, 0], along_x[:, 1], along_x[:, 2], bed_x, spacing, 2)
    mass_y, north_y, east_y = sweep_axis(along_y[:, 0], along_y[:, 2], along_y[:, 1], bed_y, spacing, 1)
    depth = field[:, 0]
    east_flow = field[:, 1]
    north_flow = field[:, 2]
    drag = GRAVITY * roughness * roughness * jnp.sqrt(east_flow * east_flow + north_flow * north_flow) / depth ** (7.0 / 3.0)
    return jnp.stack([mass_x + mass_y, east_x + east_y - drag * east_flow, north_x + north_y - drag * north_flow], axis=1)

def spacing_of(levels):
    return jnp.where(levels == 0, COARSE_SPACING, jnp.where(levels == 1, COARSE_SPACING / 2, COARSE_SPACING / 4)).astype(jnp.float32)[:, None, None]

def reference(old_state, bed, roughness, levels, sources, neighbours, face_codes, step_index):
    state = jnp.take(old_state, sources, axis=0)
    total = state.shape[0]
    opposite = jnp.array([1, 0, 3, 2], jnp.int32)
    first_index = jnp.maximum(neighbours[:, 0::2], 0) * 4 + opposite[None, :]
    second_index = jnp.maximum(neighbours[:, 1::2], 0) * 4 + opposite[None, :]
    flow_signs = jnp.array([[1.0, -1.0, 1.0], [1.0, -1.0, 1.0], [1.0, 1.0, -1.0], [1.0, 1.0, -1.0]], jnp.float32)
    bed_signs = jnp.ones((4, 1), jnp.float32)

    def ghosts_of(field, signs):
        strips = strips_of(field)
        flat = strips.reshape((total * 4,) + strips.shape[2:])
        return combine(jnp.take(flat, first_index, axis=0), jnp.take(flat, second_index, axis=0), strips, face_codes, signs)
    bed_field = bed[:, None]
    bed_x, bed_y = pad_field(bed_field, ghosts_of(bed_field, bed_signs))
    bed_x = bed_x[:, 0]
    bed_y = bed_y[:, 0]
    spacing = spacing_of(levels)
    groups = total // P_DEV

    def grouped(array):
        return array.reshape((groups, P_DEV) + array.shape[1:])

    def block_rate(items):
        return tendency(items[0], items[1], items[2], items[3], items[4], items[5])

    def evolve(field, step_size):
        ghosts = ghosts_of(field, flow_signs)
        parts = (grouped(field), grouped(ghosts), grouped(bed_x), grouped(bed_y), grouped(roughness), grouped(spacing))
        rate = lax.map(block_rate, parts).reshape(field.shape)
        return field + step_size * rate
    for step in range(STEPS):
        step_size = STEP_BASE * (2.0 + step_index[step].astype(jnp.float32)) / 5.0
        sectioned = evolve(state, step_size)
        state = 0.5 * state + 0.5 * evolve(sectioned, step_size)
    return state
```

```python
import functools

import jax
import jax.numpy as jnp
from jax import lax
from jax.experimental import pallas as pl
from jax.experimental.pallas import tpu as pltpu
from jax.sharding import PartitionSpec as P

STEPS = 3
MOVE = 8
GRAVITY = 9.81
COARSE_SPACING = 32.0
STEP_BASE = 0.15
VMEM_BYTES = 40 * 1024 * 1024
OPPOSITE = (1, 0, 3, 2)
FLIPPED = (1, 1, 2, 2)
LOW, HIGH = 8, 136


def minmod(a, b):
    return jnp.maximum(jnp.minimum(a, b), 0.0) + jnp.minimum(jnp.maximum(a, b), 0.0)


def fluxes(padded, flux, normal, tangent):
    for chunk in range(17):
        r = 8 * chunk

        def faces(q):
            v0, v1, v2, v3 = (padded[q, r + 6 + s : r + 14 + s, :] for s in range(4))
            a, b, c = v1 - v0, v2 - v1, v3 - v2
            return v1 + 0.5 * minmod(a, b), v2 - 0.5 * minmod(b, c)

        hl, hr = faces(0)
        nl, nr = faces(normal)
        tl, tr = faces(tangent)
        ul, ur = nl / hl, nr / hr
        gl, gr = GRAVITY * hl, GRAVITY * hr
        cl, cr = jnp.sqrt(gl), jnp.sqrt(gr)
        slow = jnp.minimum(jnp.minimum(ul - cl, ur - cr), 0.0)
        fast = jnp.maximum(jnp.maximum(ul + cl, ur + cr), 0.0)
        inv = 1.0 / (fast - slow)
        wl, wr, wd = fast * inv, slow * inv, fast * slow * inv
        flux[0, r : r + 8, :] = wl * nl - wr * nr + wd * (hr - hl)
        flux[1, r : r + 8, :] = (
            wl * (nl * ul + 0.5 * gl * hl) - wr * (nr * ur + 0.5 * gr * hr) + wd * (nr - nl)
        )
        flux[2, r : r + 8, :] = wl * (tl * ul) - wr * (tr * ur) + wd * (tr - tl)


def divergence(padded, flux, r):
    mass = flux[0, r + 1 : r + 9, :] - flux[0, r : r + 8, :]
    slope = padded[3, r + 9 : r + 17, :] - padded[3, r + 7 : r + 15, :]
    depth = padded[0, r + 8 : r + 16, :]
    normal = flux[1, r + 1 : r + 9, :] - flux[1, r : r + 8, :] + (0.5 * GRAVITY) * depth * slope
    tangent = flux[2, r + 1 : r + 9, :] - flux[2, r : r + 8, :]
    return mass, normal, tangent


def write_strips(fields, fields_t, strips):
    for c in range(4):
        for d in range(4):
            row = slice(4 * c + d, 4 * c + d + 1)
            strips[0][0, row, :] = fields_t(c, d)
            strips[1][0, row, :] = fields_t(c, 127 - d)
            strips[2][0, row, :] = fields(c, d)
            strips[3][0, row, :] = fields(c, 127 - d)


def write_ghosts(patch, ints, own, got, pads):
    lane = lax.broadcasted_iota(jnp.int32, (16, 128), 1)
    half = lane // 2
    even = (2 * lane) % 128
    low = lane < 64
    for f in range(4):
        opp = OPPOSITE[f]
        first = ints[0, 4 * patch + f]
        second = ints[1, 4 * patch + f]
        far = ints[2, 4 * patch + f] == 1
        code = ints[3, 4 * patch + f]
        a = jnp.where(far, got[f][first], own[opp][first])
        b = jnp.where(far, got[f][second], own[opp][second])
        index = jnp.where(
            code == 1, half, jnp.where(code == 2, half + 64, jnp.where(code == 3, even, lane))
        )
        take = functools.partial(jnp.take_along_axis, axis=1, mode="promise_in_bounds")
        a_even = take(a, index)
        odd = even + 1
        pair = jnp.where(low, a_even + take(a, odd), take(b, even) + take(b, odd))
        mine = own[f][patch]
        for c in range(4):
            for k in range(2):
                o = 4 * c + k
                same = a_even[o : o + 1]
                edge = a_even[4 * c : 4 * c + 1]
                p = 4 * c + 2 * k
                finer = 0.25 * (pair[p : p + 1] + pair[p + 1 : p + 2])
                mirror = mine[o : o + 1]
                if c == FLIPPED[f]:
                    mirror = -mirror
                value = jnp.where(
                    code == 0,
                    same,
                    jnp.where(code == 3, finer, jnp.where(code == 4, mirror, edge)),
                )
                row = (LOW - 1 - k) if f % 2 == 0 else (HIGH + k)
                pads[f // 2][c, row : row + 1, :] = value


def stage_kernel(second_stage, step, *refs):
    refs = list(refs)
    ints, floats = refs[0:2]
    state, state_t, bed, bed_t, rough = refs[2:7]
    at = 7
    base = None
    if second_stage:
        base = refs[7]
        at = 8
    own, got = refs[at : at + 4], refs[at + 4 : at + 8]
    at += 8
    last = second_stage and step == STEPS - 1
    out = refs[at]
    at += 1
    if not last:
        out_t, outs = refs[at], refs[at + 1 : at + 5]
        at += 5
    pad_x, pad_y, flux_x, flux_y, div_x = refs[at:]
    patch = pl.program_id(0)
    for c in range(3):
        pad_y[c, LOW:HIGH, :] = state[0, c]
        pad_x[c, LOW:HIGH, :] = state_t[0, c]
    pad_y[3, LOW:HIGH, :] = bed[0]
    pad_x[3, LOW:HIGH, :] = bed_t[0]
    write_ghosts(patch, ints, own, got, (pad_x, pad_y))
    fluxes(pad_x, flux_x, 1, 2)
    for chunk in range(16):
        r = 8 * chunk
        for q, value in enumerate(divergence(pad_x, flux_x, r)):
            div_x[q, r : r + 8, :] = value
    fluxes(pad_y, flux_y, 2, 1)
    for q in range(3):
        flux_x[q, 0:128, :] = div_x[q].T
    dt = floats[step]
    over = dt * floats[STEPS + patch]
    for chunk in range(16):
        r = 8 * chunk
        rows = slice(r, r + 8)
        mass, north, east = divergence(pad_y, flux_y, r)
        h, hu, hv = (state[0, c, rows, :] for c in range(3))
        n = rough[0, rows, :]
        drag = (dt * GRAVITY) * n * n * jnp.sqrt(hu * hu + hv * hv)
        drag = drag * jnp.exp((-7.0 / 3.0) * jnp.log(h))
        new = (
            h - over * (mass + flux_x[0, rows, :]),
            hu - over * (east + flux_x[1, rows, :]) - drag * hu,
            hv - over * (north + flux_x[2, rows, :]) - drag * hv,
        )
        for c in range(3):
            if second_stage:
                out[0, c, rows, :] = 0.5 * base[0, c, rows, :] + 0.5 * new[c]
            else:
                out[0, c, rows, :] = new[c]
    if not last:
        for c in range(3):
            out_t[0, c] = out[0, c].T
        write_strips(
            lambda c, d: out[0, c, d : d + 1, :] if c < 3 else bed[0, d : d + 1, :],
            lambda c, d: out_t[0, c, d : d + 1, :] if c < 3 else bed_t[0, d : d + 1, :],
            outs,
        )


def patch_spec(*shape):
    return pl.BlockSpec((1,) + shape, lambda i: (i,) + (0,) * len(shape))


def stage(second_stage, step, ints, floats, state, state_t, bed, bed_t, rough, base, own, got):
    owned = bed.shape[0]
    whole = pl.BlockSpec((owned, 16, 128), lambda i: (0, 0, 0))
    smem = pl.BlockSpec(memory_space=pltpu.SMEM)
    full, flat, strip = patch_spec(3, 128, 128), patch_spec(128, 128), patch_spec(16, 128)
    in_specs = [smem, smem, full, full, flat, flat, flat]
    args = [ints, floats, state, state_t, bed, bed_t, rough]
    if second_stage:
        in_specs.append(full)
        args.append(base)
    in_specs += [whole] * 8
    args += list(own) + list(got)
    field = jax.ShapeDtypeStruct(state.shape, jnp.float32)
    out_shape, out_specs = [field], [full]
    if not (second_stage and step == STEPS - 1):
        out_shape += [field] + [jax.ShapeDtypeStruct((owned, 16, 128), jnp.float32)] * 4
        out_specs += [full] + [strip] * 4
    scratch = [
        pltpu.VMEM((4, 152, 128), jnp.float32),
        pltpu.VMEM((4, 152, 128), jnp.float32),
        pltpu.VMEM((3, 136, 128), jnp.float32),
        pltpu.VMEM((3, 136, 128), jnp.float32),
        pltpu.VMEM((3, 128, 128), jnp.float32),
    ]
    got_out = pl.pallas_call(
        functools.partial(stage_kernel, second_stage, step),
        grid=(owned,),
        in_specs=in_specs,
        out_specs=out_specs,
        out_shape=out_shape,
        scratch_shapes=scratch,
        compiler_params=pltpu.CompilerParams(vmem_limit_bytes=VMEM_BYTES),
        name="stage",
    )(*args)
    if len(got_out) == 1:
        return got_out[0], None, None
    return got_out[0], got_out[1], got_out[2:]


def pick_patches(table, indices):
    count = indices.shape[0]

    def body(index_ref, source, out):
        out[...] = source[...]

    return pl.pallas_call(
        body,
        grid_spec=pltpu.PrefetchScalarGridSpec(
            num_scalar_prefetch=1,
            grid=(count,),
            in_specs=[pl.BlockSpec((1, 3, 128, 128), lambda i, ind: (ind[i], 0, 0, 0))],
            out_specs=pl.BlockSpec((1, 3, 128, 128), lambda i, ind: (i, 0, 0, 0)),
        ),
        out_shape=jax.ShapeDtypeStruct((count, 3, 128, 128), jnp.float32),
        name="pick",
    )(indices, table)


def assemble(picks, old_state, from_low, from_high, bed):
    owned = bed.shape[0]

    def body(picks_ref, here, low, high, bed_ref, state, state_t, bed_t, *strips):
        where = picks_ref[0, pl.program_id(0)]
        for c in range(3):
            value = jnp.where(where == 0, low[0, c], jnp.where(where == 2, high[0, c], here[0, c]))
            state[0, c] = value
            state_t[0, c] = value.T
        bed_t[0] = bed_ref[0].T
        write_strips(
            lambda c, d: state[0, c, d : d + 1, :] if c < 3 else bed_ref[0, d : d + 1, :],
            lambda c, d: state_t[0, c, d : d + 1, :] if c < 3 else bed_t[0, d : d + 1, :],
            strips,
        )

    def chosen(row):
        return pl.BlockSpec((1, 3, 128, 128), lambda i, ind: (ind[row, i], 0, 0, 0))

    def each(*shape):
        return pl.BlockSpec((1,) + shape, lambda i, ind: (i,) + (0,) * len(shape))

    field = jax.ShapeDtypeStruct((owned, 3, 128, 128), jnp.float32)
    strip = jax.ShapeDtypeStruct((owned, 16, 128), jnp.float32)
    out = pl.pallas_call(
        body,
        grid_spec=pltpu.PrefetchScalarGridSpec(
            num_scalar_prefetch=1,
            grid=(owned,),
            in_specs=[chosen(1), chosen(2), chosen(3), each(128, 128)],
            out_specs=[each(3, 128, 128), each(3, 128, 128), each(128, 128)] + [each(16, 128)] * 4,
        ),
        out_shape=[field, field, jax.ShapeDtypeStruct(bed.shape, jnp.float32)] + [strip] * 4,
        compiler_params=pltpu.CompilerParams(vmem_limit_bytes=VMEM_BYTES),
        name="assemble",
    )(picks, old_state, from_low, from_high, bed)
    return out[0], out[1], out[2], out[3:]


def shifted(value, axis, up):
    devices = lax.axis_size(axis)
    pairs = [(i, i + 1) for i in range(devices - 1)]
    return lax.ppermute(value, axis, pairs if up else [(j, i) for i, j in pairs])


def exchange(strips):
    return [
        shifted(strips[1], "gx", True),
        shifted(strips[0], "gx", False),
        shifted(strips[3], "gy", True),
        shifted(strips[2], "gy", False),
    ]


def on_device(old_state, bed, roughness, levels, sources, neighbours, face_codes, step_index):
    owned = levels.shape[0]
    capacity = old_state.shape[0]
    across = lax.axis_size("gy")
    device = lax.axis_index("gx") * across + lax.axis_index("gy")
    slots = jnp.arange(MOVE, dtype=jnp.int32)

    def ranks(mask):
        count = jnp.arange(owned)
        before = count[:, None] > count[None, :]
        return jnp.sum(jnp.where(before & mask[None, :], 1, 0), axis=1)

    def to_send(target):
        theirs = lax.dynamic_slice_in_dim(sources, target * owned, owned)
        mask = theirs // capacity == device
        hit = mask[None, :] & (ranks(mask)[None, :] == slots[:, None])
        return jnp.sum(jnp.where(hit, theirs % capacity, 0), axis=1)

    sends = jnp.concatenate([to_send(device + across), to_send(device - across)])
    picked = pick_patches(old_state, sends.astype(jnp.int32))
    from_low = shifted(picked[:MOVE], "gx", True)
    from_high = shifted(picked[MOVE:], "gx", False)

    mine = lax.dynamic_slice_in_dim(sources, device * owned, owned)
    source_dev = mine // capacity
    is_low = source_dev == device - across
    is_high = source_dev == device + across
    picks = jnp.stack(
        [
            jnp.where(is_low, 0, jnp.where(is_high, 2, 1)),
            jnp.where(is_low | is_high, 0, mine % capacity),
            jnp.where(is_low, jnp.minimum(ranks(is_low), MOVE - 1), 0),
            jnp.where(is_high, jnp.minimum(ranks(is_high), MOVE - 1), 0),
        ]
    ).astype(jnp.int32)
    state, state_t, bed_t, strips = assemble(picks, old_state, from_low, from_high, bed)

    first = jnp.maximum(neighbours[:, 0::2], 0)
    second = jnp.maximum(neighbours[:, 1::2], 0)
    far = jnp.where(first // owned != device, 1, 0)
    ints = jnp.stack(
        [(first % owned).reshape(-1), (second % owned).reshape(-1), far.reshape(-1),
         face_codes.reshape(-1)]
    ).astype(jnp.int32)
    spacing = jnp.where(
        levels == 0, COARSE_SPACING, jnp.where(levels == 1, COARSE_SPACING / 2, COARSE_SPACING / 4)
    ).astype(jnp.float32)
    step_sizes = STEP_BASE * (2.0 + step_index.astype(jnp.float32)) / 5.0
    floats = jnp.concatenate([step_sizes, 1.0 / spacing])

    for step in range(STEPS):
        base = state
        got = exchange(strips)
        section, section_t, strips = stage(
            False, step, ints, floats, state, state_t, bed, bed_t, roughness, None, strips, got
        )
        got = exchange(strips)
        state, state_t, strips = stage(
            True, step, ints, floats, section, section_t, bed, bed_t, roughness, base, strips, got
        )
    return state


def solution(mesh):
    in_specs = (
        P(("env", "gx", "gy"), None, None, None),
        P(("env", "gx", "gy"), None, None),
        P(("env", "gx", "gy"), None, None),
        P(("env", "gx", "gy")),
        P("env"),
        P(("env", "gx", "gy"), None),
        P(("env", "gx", "gy"), None),
        P("env"),
    )
    out_specs = P(("env", "gx", "gy"), None, None, None)
    return jax.shard_map(
        on_device, mesh=mesh, in_specs=in_specs, out_specs=out_specs, check_vma=False
    )
```

```python
import functools

import jax
import jax.numpy as jnp
from jax import lax
from jax.experimental import pallas as pl
from jax.experimental.pallas import tpu as pltpu
from jax.sharding import PartitionSpec as P

STEPS = 3
MOVE = 8
GRAVITY = 9.81
COARSE_SPACING = 32.0
STEP_BASE = 0.15
VMEM_BYTES = 40 * 1024 * 1024
OPPOSITE = (1, 0, 3, 2)
FLIPPED = (1, 1, 2, 2)
LOW, HIGH = 8, 136


def minmod(a, b):
    return jnp.maximum(jnp.minimum(a, b), 0.0) + jnp.minimum(jnp.maximum(a, b), 0.0)


def fluxes(padded, flux, normal, tangent):
    for chunk in range(17):
        r = 8 * chunk

        def faces(q):
            v0, v1, v2, v3 = (padded[q, r + 6 + s : r + 14 + s, :] for s in range(4))
            a, b, c = v1 - v0, v2 - v1, v3 - v2
            return v1 + 0.5 * minmod(a, b), v2 - 0.5 * minmod(b, c)

        hl, hr = faces(0)
        nl, nr = faces(normal)
        tl, tr = faces(tangent)
        ul, ur = nl / hl, nr / hr
        gl, gr = GRAVITY * hl, GRAVITY * hr
        cl, cr = jnp.sqrt(gl), jnp.sqrt(gr)
        slow = jnp.minimum(jnp.minimum(ul - cl, ur - cr), 0.0)
        fast = jnp.maximum(jnp.maximum(ul + cl, ur + cr), 0.0)
        inv = 1.0 / (fast - slow)
        wl, wr, wd = fast * inv, slow * inv, fast * slow * inv
        flux[0, r : r + 8, :] = wl * nl - wr * nr + wd * (hr - hl)
        flux[1, r : r + 8, :] = (
            wl * (nl * ul + 0.5 * gl * hl) - wr * (nr * ur + 0.5 * gr * hr) + wd * (nr - nl)
        )
        flux[2, r : r + 8, :] = wl * (tl * ul) - wr * (tr * ur) + wd * (tr - tl)


def divergence(padded, flux, r):
    mass = flux[0, r + 1 : r + 9, :] - flux[0, r : r + 8, :]
    slope = padded[3, r + 9 : r + 17, :] - padded[3, r + 7 : r + 15, :]
    depth = padded[0, r + 8 : r + 16, :]
    normal = flux[1, r + 1 : r + 9, :] - flux[1, r : r + 8, :] + (0.5 * GRAVITY) * depth * slope
    tangent = flux[2, r + 1 : r + 9, :] - flux[2, r : r + 8, :]
    return mass, normal, tangent


def write_strips(fields, fields_t, strips):
    for c in range(4):
        for d in range(4):
            row = slice(4 * c + d, 4 * c + d + 1)
            strips[0][0, row, :] = fields_t(c, d)
            strips[1][0, row, :] = fields_t(c, 127 - d)
            strips[2][0, row, :] = fields(c, d)
            strips[3][0, row, :] = fields(c, 127 - d)


def write_ghosts(patch, ints, own, got, pads):
    lane = lax.broadcasted_iota(jnp.int32, (16, 128), 1)
    half = lane // 2
    even = (2 * lane) % 128
    low = lane < 64
    for f in range(4):
        opp = OPPOSITE[f]
        first = ints[0, 4 * patch + f]
        second = ints[1, 4 * patch + f]
        far = ints[2, 4 * patch + f] == 1
        code = ints[3, 4 * patch + f]
        a = jnp.where(far, got[f][first], own[opp][first])
        b = jnp.where(far, got[f][second], own[opp][second])
        index = jnp.where(
            code == 1, half, jnp.where(code == 2, half + 64, jnp.where(code == 3, even, lane))
        )
        take = functools.partial(jnp.take_along_axis, axis=1, mode="promise_in_bounds")
        a_even = take(a, index)
        odd = even + 1
        pair = jnp.where(low, a_even + take(a, odd), take(b, even) + take(b, odd))
        mine = own[f][patch]
        for c in range(4):
            for k in range(2):
                o = 4 * c + k
                same = a_even[o : o + 1]
                edge = a_even[4 * c : 4 * c + 1]
                p = 4 * c + 2 * k
                finer = 0.25 * (pair[p : p + 1] + pair[p + 1 : p + 2])
                mirror = mine[o : o + 1]
                if c == FLIPPED[f]:
                    mirror = -mirror
                value = jnp.where(
                    code == 0,
                    same,
                    jnp.where(code == 3, finer, jnp.where(code == 4, mirror, edge)),
                )
                row = (LOW - 1 - k) if f % 2 == 0 else (HIGH + k)
                pads[f // 2][c, row : row + 1, :] = value


def stage_kernel(second_stage, step, *refs):
    refs = list(refs)
    ints, floats = refs[0:2]
    state, state_t, bed, bed_t, rough = refs[2:7]
    at = 7
    base = None
    if second_stage:
        base = refs[7]
        at = 8
    own, got = refs[at : at + 4], refs[at + 4 : at + 8]
    at += 8
    last = second_stage and step == STEPS - 1
    out = refs[at]
    at += 1
    if not last:
        out_t, outs = refs[at], refs[at + 1 : at + 5]
        at += 5
    pad_x, pad_y, flux_x, flux_y, div_x = refs[at:]
    patch = pl.program_id(0)
    for c in range(3):
        pad_y[c, LOW:HIGH, :] = state[0, c]
        pad_x[c, LOW:HIGH, :] = state_t[0, c]
    pad_y[3, LOW:HIGH, :] = bed[0]
    pad_x[3, LOW:HIGH, :] = bed_t[0]
    write_ghosts(patch, ints, own, got, (pad_x, pad_y))
    fluxes(pad_x, flux_x, 1, 2)
    for chunk in range(16):
        r = 8 * chunk
        for q, value in enumerate(divergence(pad_x, flux_x, r)):
            div_x[q, r : r + 8, :] = value
    fluxes(pad_y, flux_y, 2, 1)
    for q in range(3):
        flux_x[q, 0:128, :] = div_x[q].T
    dt = floats[step]
    over = dt * floats[STEPS + patch]
    for chunk in range(16):
        r = 8 * chunk
        rows = slice(r, r + 8)
        mass, north, east = divergence(pad_y, flux_y, r)
        h, hu, hv = (state[0, c, rows, :] for c in range(3))
        n = rough[0, rows, :]
        drag = (dt * GRAVITY) * n * n * jnp.sqrt(hu * hu + hv * hv)
        drag = drag * jnp.exp((-7.0 / 3.0) * jnp.log(h))
        new = (
            h - over * (mass + flux_x[0, rows, :]),
            hu - over * (east + flux_x[1, rows, :]) - drag * hu,
            hv - over * (north + flux_x[2, rows, :]) - drag * hv,
        )
        for c in range(3):
            if second_stage:
                out[0, c, rows, :] = 0.5 * base[0, c, rows, :] + 0.5 * new[c]
            else:
                out[0, c, rows, :] = new[c]
    if not last:
        for c in range(3):
            out_t[0, c] = out[0, c].T
        write_strips(
            lambda c, d: out[0, c, d : d + 1, :] if c < 3 else bed[0, d : d + 1, :],
            lambda c, d: out_t[0, c, d : d + 1, :] if c < 3 else bed_t[0, d : d + 1, :],
            outs,
        )


def patch_spec(*shape):
    return pl.BlockSpec((1,) + shape, lambda i: (i,) + (0,) * len(shape))


def stage(second_stage, step, ints, floats, state, state_t, bed, bed_t, rough, base, own, got):
    owned = bed.shape[0]
    whole = pl.BlockSpec((owned, 16, 128), lambda i: (0, 0, 0))
    smem = pl.BlockSpec(memory_space=pltpu.SMEM)
    full, flat, strip = patch_spec(3, 128, 128), patch_spec(128, 128), patch_spec(16, 128)
    in_specs = [smem, smem, full, full, flat, flat, flat]
    args = [ints, floats, state, state_t, bed, bed_t, rough]
    if second_stage:
        in_specs.append(full)
        args.append(base)
    in_specs += [whole] * 8
    args += list(own) + list(got)
    field = jax.ShapeDtypeStruct(state.shape, jnp.float32)
    out_shape, out_specs = [field], [full]
    if not (second_stage and step == STEPS - 1):
        out_shape += [field] + [jax.ShapeDtypeStruct((owned, 16, 128), jnp.float32)] * 4
        out_specs += [full] + [strip] * 4
    scratch = [
        pltpu.VMEM((4, 152, 128), jnp.float32),
        pltpu.VMEM((4, 152, 128), jnp.float32),
        pltpu.VMEM((3, 136, 128), jnp.float32),
        pltpu.VMEM((3, 136, 128), jnp.float32),
        pltpu.VMEM((3, 128, 128), jnp.float32),
    ]
    got_out = pl.pallas_call(
        functools.partial(stage_kernel, second_stage, step),
        grid=(owned,),
        in_specs=in_specs,
        out_specs=out_specs,
        out_shape=out_shape,
        scratch_shapes=scratch,
        compiler_params=pltpu.CompilerParams(vmem_limit_bytes=VMEM_BYTES),
        name="stage",
    )(*args)
    if len(got_out) == 1:
        return got_out[0], None, None
    return got_out[0], got_out[1], got_out[2:]


def sends_of(axis):
    index, devices = lax.axis_index(axis), lax.axis_size(axis)
    up = ({axis: lax.rem(index + 1, devices)}, index < devices - 1, index > 0)
    down = ({axis: lax.rem(index + devices - 1, devices)}, index > 0, index < devices - 1)
    return up, down


def greet(links):
    barrier = pltpu.get_barrier_semaphore()
    for target, sends, _ in links:

        @pl.when(sends)
        def _(target=target):
            pl.semaphore_signal(
                barrier, inc=1, device_id=target, device_id_type=pl.DeviceIdType.MESH
            )

    pl.semaphore_wait(barrier, sum(sends.astype(jnp.int32) for _, sends, _ in links))


def remote(source, target, send_sem, recv_sem, link):
    return pltpu.make_async_remote_copy(
        src_ref=source,
        dst_ref=target,
        send_sem=send_sem,
        recv_sem=recv_sem,
        device_id=link[0],
        device_id_type=pl.DeviceIdType.MESH,
    )


def finish(copies):
    for copy, link in copies:
        pl.when(link[2])(copy.wait_recv)
    for copy, link in copies:
        pl.when(link[1])(copy.wait_send)


def exchange_kernel(west, east, south, north, *refs):
    got, send_sem, recv_sem = refs[:4], refs[4], refs[5]
    links = sends_of("gx") + sends_of("gy")
    greet(links)
    copies = []
    for d, source in enumerate((east, west, north, south)):
        copy = remote(source, got[d], send_sem.at[d], recv_sem.at[d], links[d])
        pl.when(links[d][1])(copy.start)
        copies.append((copy, links[d]))
    finish(copies)


def exchange(strips):
    anywhere = pl.BlockSpec(memory_space=pl.ANY)
    return pl.pallas_call(
        exchange_kernel,
        in_specs=[anywhere] * 4,
        out_specs=[anywhere] * 4,
        out_shape=[jax.ShapeDtypeStruct(strips[0].shape, jnp.float32)] * 4,
        scratch_shapes=[pltpu.SemaphoreType.DMA((4,)), pltpu.SemaphoreType.DMA((4,))],
        compiler_params=pltpu.CompilerParams(collective_id=0, has_side_effects=True),
        name="exchange",
    )(*strips)


PIECE = 2


def rebalance_kernel(indices, table, low, high, packed, send_sem, recv_sem):
    links = sends_of("gx")
    greet(links)
    copies = []
    for piece in range(MOVE // PIECE):
        for d, target in enumerate((low, high)):
            begin = piece * PIECE
            for k in range(PIECE):
                packed[d * MOVE + begin + k] = table[indices[d * MOVE + begin + k]]
            n = d * (MOVE // PIECE) + piece
            copy = remote(
                packed.at[pl.ds(d * MOVE + begin, PIECE)],
                target.at[pl.ds(begin, PIECE)],
                send_sem.at[n],
                recv_sem.at[n],
                links[d],
            )
            pl.when(links[d][1])(copy.start)
            copies.append((copy, links[d]))
    finish(copies)


def rebalance(table, indices):
    anywhere = pl.BlockSpec(memory_space=pl.ANY)
    pieces = 2 * (MOVE // PIECE)
    patch = table.shape[1:]
    return pl.pallas_call(
        rebalance_kernel,
        in_specs=[pl.BlockSpec(memory_space=pltpu.SMEM), pl.BlockSpec(memory_space=pltpu.VMEM)],
        out_specs=[anywhere] * 2,
        out_shape=[jax.ShapeDtypeStruct((MOVE,) + patch, jnp.float32)] * 2,
        scratch_shapes=[
            pltpu.VMEM((2 * MOVE,) + patch, jnp.float32),
            pltpu.SemaphoreType.DMA((pieces,)),
            pltpu.SemaphoreType.DMA((pieces,)),
        ],
        compiler_params=pltpu.CompilerParams(
            collective_id=1, has_side_effects=True, vmem_limit_bytes=VMEM_BYTES
        ),
        name="rebalance",
    )(indices, table)


def assemble(picks, old_state, from_low, from_high, bed):
    owned = bed.shape[0]

    def body(picks_ref, here, low, high, bed_ref, state, state_t, bed_t, *strips):
        where = picks_ref[0, pl.program_id(0)]
        for c in range(3):
            value = jnp.where(where == 0, low[0, c], jnp.where(where == 2, high[0, c], here[0, c]))
            state[0, c] = value
            state_t[0, c] = value.T
        bed_t[0] = bed_ref[0].T
        write_strips(
            lambda c, d: state[0, c, d : d + 1, :] if c < 3 else bed_ref[0, d : d + 1, :],
            lambda c, d: state_t[0, c, d : d + 1, :] if c < 3 else bed_t[0, d : d + 1, :],
            strips,
        )

    def chosen(row):
        return pl.BlockSpec((1, 3, 128, 128), lambda i, ind: (ind[row, i], 0, 0, 0))

    def each(*shape):
        return pl.BlockSpec((1,) + shape, lambda i, ind: (i,) + (0,) * len(shape))

    field = jax.ShapeDtypeStruct((owned, 3, 128, 128), jnp.float32)
    strip = jax.ShapeDtypeStruct((owned, 16, 128), jnp.float32)
    out = pl.pallas_call(
        body,
        grid_spec=pltpu.PrefetchScalarGridSpec(
            num_scalar_prefetch=1,
            grid=(owned,),
            in_specs=[chosen(1), chosen(2), chosen(3), each(128, 128)],
            out_specs=[each(3, 128, 128), each(3, 128, 128), each(128, 128)] + [each(16, 128)] * 4,
        ),
        out_shape=[field, field, jax.ShapeDtypeStruct(bed.shape, jnp.float32)] + [strip] * 4,
        compiler_params=pltpu.CompilerParams(vmem_limit_bytes=VMEM_BYTES),
        name="assemble",
    )(picks, old_state, from_low, from_high, bed)
    return out[0], out[1], out[2], out[3:]


def on_device(old_state, bed, roughness, levels, sources, neighbours, face_codes, step_index):
    owned = levels.shape[0]
    capacity = old_state.shape[0]
    across = lax.axis_size("gy")
    device = lax.axis_index("gx") * across + lax.axis_index("gy")
    slots = jnp.arange(MOVE, dtype=jnp.int32)

    def ranks(mask):
        count = jnp.arange(owned)
        before = count[:, None] > count[None, :]
        return jnp.sum(jnp.where(before & mask[None, :], 1, 0), axis=1)

    def to_send(target):
        theirs = lax.dynamic_slice_in_dim(sources, target * owned, owned)
        mask = theirs // capacity == device
        hit = mask[None, :] & (ranks(mask)[None, :] == slots[:, None])
        return jnp.sum(jnp.where(hit, theirs % capacity, 0), axis=1)

    sends = jnp.concatenate([to_send(device + across), to_send(device - across)])
    from_low, from_high = rebalance(old_state, sends.astype(jnp.int32))

    mine = lax.dynamic_slice_in_dim(sources, device * owned, owned)
    source_dev = mine // capacity
    is_low = source_dev == device - across
    is_high = source_dev == device + across
    picks = jnp.stack(
        [
            jnp.where(is_low, 0, jnp.where(is_high, 2, 1)),
            jnp.where(is_low | is_high, 0, mine % capacity),
            jnp.where(is_low, jnp.minimum(ranks(is_low), MOVE - 1), 0),
            jnp.where(is_high, jnp.minimum(ranks(is_high), MOVE - 1), 0),
        ]
    ).astype(jnp.int32)
    state, state_t, bed_t, strips = assemble(picks, old_state, from_low, from_high, bed)

    first = jnp.maximum(neighbours[:, 0::2], 0)
    second = jnp.maximum(neighbours[:, 1::2], 0)
    far = jnp.where(first // owned != device, 1, 0)
    ints = jnp.stack(
        [(first % owned).reshape(-1), (second % owned).reshape(-1), far.reshape(-1),
         face_codes.reshape(-1)]
    ).astype(jnp.int32)
    spacing = jnp.where(
        levels == 0, COARSE_SPACING, jnp.where(levels == 1, COARSE_SPACING / 2, COARSE_SPACING / 4)
    ).astype(jnp.float32)
    step_sizes = STEP_BASE * (2.0 + step_index.astype(jnp.float32)) / 5.0
    floats = jnp.concatenate([step_sizes, 1.0 / spacing])

    for step in range(STEPS):
        base = state
        got = exchange(strips)
        section, section_t, strips = stage(
            False, step, ints, floats, state, state_t, bed, bed_t, roughness, None, strips, got
        )
        got = exchange(strips)
        state, state_t, strips = stage(
            True, step, ints, floats, section, section_t, bed, bed_t, roughness, base, strips, got
        )
    return state


def solution(mesh):
    in_specs = (
        P(("env", "gx", "gy"), None, None, None),
        P(("env", "gx", "gy"), None, None),
        P(("env", "gx", "gy"), None, None),
        P(("env", "gx", "gy")),
        P("env"),
        P(("env", "gx", "gy"), None),
        P(("env", "gx", "gy"), None),
        P("env"),
    )
    out_specs = P(("env", "gx", "gy"), None, None, None)
    return jax.shard_map(
        on_device, mesh=mesh, in_specs=in_specs, out_specs=out_specs, check_vma=False
    )
```

```python
import functools

import jax
import jax.numpy as jnp
from jax import lax
from jax.experimental import pallas as pl
from jax.experimental.pallas import tpu as pltpu
from jax.sharding import PartitionSpec as P

STEPS = 3
MOVE = 8
GRAVITY = 9.81
COARSE_SPACING = 32.0
STEP_BASE = 0.15
OPPOSITE = (1, 0, 3, 2)
FLIPPED = (1, 1, 2, 2)
LOW, HIGH = 8, 136


def minmod(a, b):
    return jnp.maximum(jnp.minimum(a, b), 0.0) + jnp.minimum(jnp.maximum(a, b), 0.0)


def fluxes(padded, flux, normal, tangent):
    for chunk in range(17):
        r = 8 * chunk

        def faces(q):
            v0, v1, v2, v3 = (padded[q, r + 6 + s : r + 14 + s, :] for s in range(4))
            a, b, c = v1 - v0, v2 - v1, v3 - v2
            return v1 + 0.5 * minmod(a, b), v2 - 0.5 * minmod(b, c)

        hl, hr = faces(0)
        nl, nr = faces(normal)
        tl, tr = faces(tangent)
        ul, ur = nl / hl, nr / hr
        gl, gr = GRAVITY * hl, GRAVITY * hr
        cl, cr = jnp.sqrt(gl), jnp.sqrt(gr)
        slow = jnp.minimum(jnp.minimum(ul - cl, ur - cr), 0.0)
        fast = jnp.maximum(jnp.maximum(ul + cl, ur + cr), 0.0)
        inv = 1.0 / (fast - slow)
        wl, wr, wd = fast * inv, slow * inv, fast * slow * inv
        flux[0, r : r + 8, :] = wl * nl - wr * nr + wd * (hr - hl)
        flux[1, r : r + 8, :] = (
            wl * (nl * ul + 0.5 * gl * hl) - wr * (nr * ur + 0.5 * gr * hr) + wd * (nr - nl)
        )
        flux[2, r : r + 8, :] = wl * (tl * ul) - wr * (tr * ur) + wd * (tr - tl)


def divergence(padded, flux, r):
    mass = flux[0, r + 1 : r + 9, :] - flux[0, r : r + 8, :]
    slope = padded[3, r + 9 : r + 17, :] - padded[3, r + 7 : r + 15, :]
    depth = padded[0, r + 8 : r + 16, :]
    normal = flux[1, r + 1 : r + 9, :] - flux[1, r : r + 8, :] + (0.5 * GRAVITY) * depth * slope
    tangent = flux[2, r + 1 : r + 9, :] - flux[2, r : r + 8, :]
    return mass, normal, tangent


def write_strips(fields, fields_t, strips):
    for c in range(4):
        for d in range(4):
            row = slice(4 * c + d, 4 * c + d + 1)
            strips[0][0, row, :] = fields_t(c, d)
            strips[1][0, row, :] = fields_t(c, 127 - d)
            strips[2][0, row, :] = fields(c, d)
            strips[3][0, row, :] = fields(c, 127 - d)


def write_ghosts(patch, ints, own, got, pads):
    lane = lax.broadcasted_iota(jnp.int32, (16, 128), 1)
    half = lane // 2
    even = (2 * lane) % 128
    low = lane < 64
    for f in range(4):
        opp = OPPOSITE[f]
        first = ints[0, 4 * patch + f]
        second = ints[1, 4 * patch + f]
        far = ints[2, 4 * patch + f] == 1
        code = ints[3, 4 * patch + f]
        a = jnp.where(far, got[f][first], own[opp][first])
        b = jnp.where(far, got[f][second], own[opp][second])
        index = jnp.where(
            code == 1, half, jnp.where(code == 2, half + 64, jnp.where(code == 3, even, lane))
        )
        take = functools.partial(jnp.take_along_axis, axis=1, mode="promise_in_bounds")
        a_even = take(a, index)
        odd = even + 1
        pair = jnp.where(low, a_even + take(a, odd), take(b, even) + take(b, odd))
        mine = own[f][patch]
        for c in range(4):
            for k in range(2):
                o = 4 * c + k
                same = a_even[o : o + 1]
                edge = a_even[4 * c : 4 * c + 1]
                p = 4 * c + 2 * k
                finer = 0.25 * (pair[p : p + 1] + pair[p + 1 : p + 2])
                mirror = mine[o : o + 1]
                if c == FLIPPED[f]:
                    mirror = -mirror
                value = jnp.where(
                    code == 0,
                    same,
                    jnp.where(code == 3, finer, jnp.where(code == 4, mirror, edge)),
                )
                row = (LOW - 1 - k) if f % 2 == 0 else (HIGH + k)
                pads[f // 2][c, row : row + 1, :] = value


def stage_kernel(second_stage, step, *refs):
    refs = list(refs)
    ints, floats = refs[0:2]
    state, state_t, bed, bed_t, rough = refs[2:7]
    at = 7
    base = None
    if second_stage:
        base = refs[7]
        at = 8
    own, got = refs[at : at + 4], refs[at + 4 : at + 8]
    at += 8
    last = second_stage and step == STEPS - 1
    out = refs[at]
    at += 1
    if not last:
        out_t, outs = refs[at], refs[at + 1 : at + 5]
        at += 5
    pad_x, pad_y, flux_x, flux_y, div_x = refs[at:]
    patch = pl.program_id(0)
    for c in range(3):
        pad_y[c, LOW:HIGH, :] = state[0, c]
        pad_x[c, LOW:HIGH, :] = state_t[0, c]
    pad_y[3, LOW:HIGH, :] = bed[0]
    pad_x[3, LOW:HIGH, :] = bed_t[0]
    write_ghosts(patch, ints, own, got, (pad_x, pad_y))
    fluxes(pad_x, flux_x, 1, 2)
    for chunk in range(16):
        r = 8 * chunk
        for q, value in enumerate(divergence(pad_x, flux_x, r)):
            div_x[q, r : r + 8, :] = value
    fluxes(pad_y, flux_y, 2, 1)
    for q in range(3):
        flux_x[q, 0:128, :] = div_x[q].T
    dt = floats[step]
    over = dt * floats[STEPS + patch]
    for chunk in range(16):
        r = 8 * chunk
        rows = slice(r, r + 8)
        mass, north, east = divergence(pad_y, flux_y, r)
        h, hu, hv = (state[0, c, rows, :] for c in range(3))
        n = rough[0, rows, :]
        drag = (dt * GRAVITY) * n * n * jnp.sqrt(hu * hu + hv * hv)
        drag = drag * jnp.exp((-7.0 / 3.0) * jnp.log(h))
        new = (
            h - over * (mass + flux_x[0, rows, :]),
            hu - over * (east + flux_x[1, rows, :]) - drag * hu,
            hv - over * (north + flux_x[2, rows, :]) - drag * hv,
        )
        for c in range(3):
            if second_stage:
                out[0, c, rows, :] = 0.5 * base[0, c, rows, :] + 0.5 * new[c]
            else:
                out[0, c, rows, :] = new[c]
    if not last:
        for c in range(3):
            out_t[0, c] = out[0, c].T
        write_strips(
            lambda c, d: out[0, c, d : d + 1, :] if c < 3 else bed[0, d : d + 1, :],
            lambda c, d: out_t[0, c, d : d + 1, :] if c < 3 else bed_t[0, d : d + 1, :],
            outs,
        )


def patch_spec(*shape):
    return pl.BlockSpec((1,) + shape, lambda i: (i,) + (0,) * len(shape))


def stage(second_stage, step, ints, floats, state, state_t, bed, bed_t, rough, base, own, got):
    owned = bed.shape[0]
    whole = pl.BlockSpec((owned, 16, 128), lambda i: (0, 0, 0))
    smem = pl.BlockSpec(memory_space=pltpu.SMEM)
    full, flat, strip = patch_spec(3, 128, 128), patch_spec(128, 128), patch_spec(16, 128)
    in_specs = [smem, smem, full, full, flat, flat, flat]
    args = [ints, floats, state, state_t, bed, bed_t, rough]
    if second_stage:
        in_specs.append(full)
        args.append(base)
    in_specs += [whole] * 8
    args += list(own) + list(got)
    field = jax.ShapeDtypeStruct(state.shape, jnp.float32)
    out_shape, out_specs = [field], [full]
    if not (second_stage and step == STEPS - 1):
        out_shape += [field] + [jax.ShapeDtypeStruct((owned, 16, 128), jnp.float32)] * 4
        out_specs += [full] + [strip] * 4
    scratch = [
        pltpu.VMEM((4, 152, 128), jnp.float32),
        pltpu.VMEM((4, 152, 128), jnp.float32),
        pltpu.VMEM((3, 136, 128), jnp.float32),
        pltpu.VMEM((3, 136, 128), jnp.float32),
        pltpu.VMEM((3, 128, 128), jnp.float32),
    ]
    got_out = pl.pallas_call(
        functools.partial(stage_kernel, second_stage, step),
        grid=(owned,),
        in_specs=in_specs,
        out_specs=out_specs,
        out_shape=out_shape,
        scratch_shapes=scratch,
        name="stage",
    )(*args)
    if len(got_out) == 1:
        return got_out[0], None, None
    return got_out[0], got_out[1], got_out[2:]


def sends_of(axis):
    index, devices = lax.axis_index(axis), lax.axis_size(axis)
    up = ({axis: lax.rem(index + 1, devices)}, index < devices - 1, index > 0)
    down = ({axis: lax.rem(index + devices - 1, devices)}, index > 0, index < devices - 1)
    return up, down


def greet(links):
    barrier = pltpu.get_barrier_semaphore()
    for target, sends, _ in links:

        @pl.when(sends)
        def _(target=target):
            pl.semaphore_signal(
                barrier, inc=1, device_id=target, device_id_type=pl.DeviceIdType.MESH
            )

    pl.semaphore_wait(barrier, sum(sends.astype(jnp.int32) for _, sends, _ in links))


def remote(source, target, send_sem, recv_sem, link):
    return pltpu.make_async_remote_copy(
        src_ref=source,
        dst_ref=target,
        send_sem=send_sem,
        recv_sem=recv_sem,
        device_id=link[0],
        device_id_type=pl.DeviceIdType.MESH,
    )


def finish(copies):
    for copy, link in copies:
        pl.when(link[2])(copy.wait_recv)
    for copy, link in copies:
        pl.when(link[1])(copy.wait_send)


def exchange_kernel(west, east, south, north, *refs):
    got, send_sem, recv_sem = refs[:4], refs[4], refs[5]
    links = sends_of("gx") + sends_of("gy")
    greet(links)
    copies = []
    for d, source in enumerate((east, west, north, south)):
        copy = remote(source, got[d], send_sem.at[d], recv_sem.at[d], links[d])
        pl.when(links[d][1])(copy.start)
        copies.append((copy, links[d]))
    finish(copies)


def exchange(strips):
    anywhere = pl.BlockSpec(memory_space=pl.ANY)
    return pl.pallas_call(
        exchange_kernel,
        in_specs=[anywhere] * 4,
        out_specs=[anywhere] * 4,
        out_shape=[jax.ShapeDtypeStruct(strips[0].shape, jnp.float32)] * 4,
        scratch_shapes=[pltpu.SemaphoreType.DMA((4,)), pltpu.SemaphoreType.DMA((4,))],
        compiler_params=pltpu.CompilerParams(collective_id=0, has_side_effects=True),
        name="exchange",
    )(*strips)


PIECE = 2


def rebalance_kernel(indices, table, low, high, packed, send_sem, recv_sem):
    links = sends_of("gx")
    greet(links)
    copies = []
    for piece in range(MOVE // PIECE):
        for d, target in enumerate((low, high)):
            begin = piece * PIECE
            for k in range(PIECE):
                packed[d * MOVE + begin + k] = table[indices[d * MOVE + begin + k]]
            n = d * (MOVE // PIECE) + piece
            copy = remote(
                packed.at[pl.ds(d * MOVE + begin, PIECE)],
                target.at[pl.ds(begin, PIECE)],
                send_sem.at[n],
                recv_sem.at[n],
                links[d],
            )
            pl.when(links[d][1])(copy.start)
            copies.append((copy, links[d]))
    finish(copies)


def rebalance(table, indices):
    anywhere = pl.BlockSpec(memory_space=pl.ANY)
    pieces = 2 * (MOVE // PIECE)
    patch = table.shape[1:]
    return pl.pallas_call(
        rebalance_kernel,
        in_specs=[pl.BlockSpec(memory_space=pltpu.SMEM), pl.BlockSpec(memory_space=pltpu.VMEM)],
        out_specs=[anywhere] * 2,
        out_shape=[jax.ShapeDtypeStruct((MOVE,) + patch, jnp.float32)] * 2,
        scratch_shapes=[
            pltpu.VMEM((2 * MOVE,) + patch, jnp.float32),
            pltpu.SemaphoreType.DMA((pieces,)),
            pltpu.SemaphoreType.DMA((pieces,)),
        ],
        compiler_params=pltpu.CompilerParams(collective_id=1, has_side_effects=True),
        name="rebalance",
    )(indices, table)


def assemble(picks, old_state, from_low, from_high, bed):
    owned = bed.shape[0]

    def body(picks_ref, here, low, high, bed_ref, state, state_t, bed_t, *strips):
        where = picks_ref[0, pl.program_id(0)]
        for c in range(3):
            value = jnp.where(where == 0, low[0, c], jnp.where(where == 2, high[0, c], here[0, c]))
            state[0, c] = value
            state_t[0, c] = value.T
        bed_t[0] = bed_ref[0].T
        write_strips(
            lambda c, d: state[0, c, d : d + 1, :] if c < 3 else bed_ref[0, d : d + 1, :],
            lambda c, d: state_t[0, c, d : d + 1, :] if c < 3 else bed_t[0, d : d + 1, :],
            strips,
        )

    def chosen(row):
        return pl.BlockSpec((1, 3, 128, 128), lambda i, ind: (ind[row, i], 0, 0, 0))

    def each(*shape):
        return pl.BlockSpec((1,) + shape, lambda i, ind: (i,) + (0,) * len(shape))

    field = jax.ShapeDtypeStruct((owned, 3, 128, 128), jnp.float32)
    strip = jax.ShapeDtypeStruct((owned, 16, 128), jnp.float32)
    out = pl.pallas_call(
        body,
        grid_spec=pltpu.PrefetchScalarGridSpec(
            num_scalar_prefetch=1,
            grid=(owned,),
            in_specs=[chosen(1), chosen(2), chosen(3), each(128, 128)],
            out_specs=[each(3, 128, 128), each(3, 128, 128), each(128, 128)] + [each(16, 128)] * 4,
        ),
        out_shape=[field, field, jax.ShapeDtypeStruct(bed.shape, jnp.float32)] + [strip] * 4,
        name="assemble",
    )(picks, old_state, from_low, from_high, bed)
    return out[0], out[1], out[2], out[3:]


def on_device(old_state, bed, roughness, levels, sources, neighbours, face_codes, step_index):
    owned = levels.shape[0]
    capacity = old_state.shape[0]
    across = lax.axis_size("gy")
    device = lax.axis_index("gx") * across + lax.axis_index("gy")
    slots = jnp.arange(MOVE, dtype=jnp.int32)

    def ranks(mask):
        count = jnp.arange(owned)
        before = count[:, None] > count[None, :]
        return jnp.sum(jnp.where(before & mask[None, :], 1, 0), axis=1)

    def to_send(target):
        theirs = lax.dynamic_slice_in_dim(sources, target * owned, owned)
        mask = theirs // capacity == device
        hit = mask[None, :] & (ranks(mask)[None, :] == slots[:, None])
        return jnp.sum(jnp.where(hit, theirs % capacity, 0), axis=1)

    sends = jnp.concatenate([to_send(device + across), to_send(device - across)])
    from_low, from_high = rebalance(old_state, sends.astype(jnp.int32))

    mine = lax.dynamic_slice_in_dim(sources, device * owned, owned)
    source_dev = mine // capacity
    is_low = source_dev == device - across
    is_high = source_dev == device + across
    picks = jnp.stack(
        [
            jnp.where(is_low, 0, jnp.where(is_high, 2, 1)),
            jnp.where(is_low | is_high, 0, mine % capacity),
            jnp.where(is_low, jnp.minimum(ranks(is_low), MOVE - 1), 0),
            jnp.where(is_high, jnp.minimum(ranks(is_high), MOVE - 1), 0),
        ]
    ).astype(jnp.int32)
    state, state_t, bed_t, strips = assemble(picks, old_state, from_low, from_high, bed)

    first = jnp.maximum(neighbours[:, 0::2], 0)
    second = jnp.maximum(neighbours[:, 1::2], 0)
    far = jnp.where(first // owned != device, 1, 0)
    ints = jnp.stack(
        [(first % owned).reshape(-1), (second % owned).reshape(-1), far.reshape(-1),
         face_codes.reshape(-1)]
    ).astype(jnp.int32)
    spacing = jnp.where(
        levels == 0, COARSE_SPACING, jnp.where(levels == 1, COARSE_SPACING / 2, COARSE_SPACING / 4)
    ).astype(jnp.float32)
    step_sizes = STEP_BASE * (2.0 + step_index.astype(jnp.float32)) / 5.0
    floats = jnp.concatenate([step_sizes, 1.0 / spacing])

    for step in range(STEPS):
        base = state
        got = exchange(strips)
        section, section_t, strips = stage(
            False, step, ints, floats, state, state_t, bed, bed_t, roughness, None, strips, got
        )
        got = exchange(strips)
        state, state_t, strips = stage(
            True, step, ints, floats, section, section_t, bed, bed_t, roughness, base, strips, got
        )
    return state


def solution(mesh):
    in_specs = (
        P(("env", "gx", "gy"), None, None, None),
        P(("env", "gx", "gy"), None, None),
        P(("env", "gx", "gy"), None, None),
        P(("env", "gx", "gy")),
        P("env"),
        P(("env", "gx", "gy"), None),
        P(("env", "gx", "gy"), None),
        P("env"),
    )
    out_specs = P(("env", "gx", "gy"), None, None, None)
    return jax.shard_map(
        on_device, mesh=mesh, in_specs=in_specs, out_specs=out_specs, check_vma=False
    )
```

```python
import functools

import jax
import jax.numpy as jnp
from jax import lax
from jax.experimental import pallas as pl
from jax.experimental.pallas import tpu as pltpu
from jax.sharding import PartitionSpec as P

STEPS = 3
MOVE = 8
GRAVITY = 9.81
COARSE_SPACING = 32.0
STEP_BASE = 0.15
OPPOSITE = (1, 0, 3, 2)
FLIPPED = (1, 1, 2, 2)
LOW, HIGH = 8, 136


def minmod(a, b):
    return jnp.maximum(jnp.minimum(a, b), 0.0) + jnp.minimum(jnp.maximum(a, b), 0.0)


def fluxes(padded, flux, normal, tangent):
    for chunk in range(17):
        r = 8 * chunk

        def faces(q):
            v0, v1, v2, v3 = (padded[q, r + 6 + s : r + 14 + s, :] for s in range(4))
            a, b, c = v1 - v0, v2 - v1, v3 - v2
            return v1 + 0.5 * minmod(a, b), v2 - 0.5 * minmod(b, c)

        hl, hr = faces(0)
        nl, nr = faces(normal)
        tl, tr = faces(tangent)
        ul, ur = nl / hl, nr / hr
        gl, gr = GRAVITY * hl, GRAVITY * hr
        cl, cr = jnp.sqrt(gl), jnp.sqrt(gr)
        slow = jnp.minimum(jnp.minimum(ul - cl, ur - cr), 0.0)
        fast = jnp.maximum(jnp.maximum(ul + cl, ur + cr), 0.0)
        inv = 1.0 / (fast - slow)
        wl, wr, wd = fast * inv, slow * inv, fast * slow * inv
        flux[0, r : r + 8, :] = wl * nl - wr * nr + wd * (hr - hl)
        flux[1, r : r + 8, :] = (
            wl * (nl * ul + 0.5 * gl * hl) - wr * (nr * ur + 0.5 * gr * hr) + wd * (nr - nl)
        )
        flux[2, r : r + 8, :] = wl * (tl * ul) - wr * (tr * ur) + wd * (tr - tl)


def divergence(padded, flux, r):
    mass = flux[0, r + 1 : r + 9, :] - flux[0, r : r + 8, :]
    slope = padded[3, r + 9 : r + 17, :] - padded[3, r + 7 : r + 15, :]
    depth = padded[0, r + 8 : r + 16, :]
    normal = flux[1, r + 1 : r + 9, :] - flux[1, r : r + 8, :] + (0.5 * GRAVITY) * depth * slope
    tangent = flux[2, r + 1 : r + 9, :] - flux[2, r : r + 8, :]
    return mass, normal, tangent


def write_strips(fields, fields_t, strips):
    for c in range(4):
        for d in range(4):
            row = slice(4 * c + d, 4 * c + d + 1)
            strips[0][0, row, :] = fields_t(c, d)
            strips[1][0, row, :] = fields_t(c, 127 - d)
            strips[2][0, row, :] = fields(c, d)
            strips[3][0, row, :] = fields(c, 127 - d)


def write_ghosts(patch, ints, own, got, pads):
    lane = lax.broadcasted_iota(jnp.int32, (16, 128), 1)
    half = lane // 2
    even = (2 * lane) % 128
    low = lane < 64
    for f in range(4):
        opp = OPPOSITE[f]
        first = ints[patch, 2 * f]
        second = ints[patch, 2 * f + 1]
        far = ints[patch, 8 + 2 * f] == 1
        code = ints[patch, 16 + f]
        a = jnp.where(far, got[f][first], own[opp][first])
        b = jnp.where(far, got[f][second], own[opp][second])
        index = jnp.where(
            code == 1, half, jnp.where(code == 2, half + 64, jnp.where(code == 3, even, lane))
        )
        take = functools.partial(jnp.take_along_axis, axis=1, mode="promise_in_bounds")
        a_even = take(a, index)
        odd = even + 1
        pair = jnp.where(low, a_even + take(a, odd), take(b, even) + take(b, odd))
        mine = own[f][patch]
        for c in range(4):
            for k in range(2):
                o = 4 * c + k
                same = a_even[o : o + 1]
                edge = a_even[4 * c : 4 * c + 1]
                p = 4 * c + 2 * k
                finer = 0.25 * (pair[p : p + 1] + pair[p + 1 : p + 2])
                mirror = mine[o : o + 1]
                if c == FLIPPED[f]:
                    mirror = -mirror
                value = jnp.where(
                    code == 0,
                    same,
                    jnp.where(code == 3, finer, jnp.where(code == 4, mirror, edge)),
                )
                row = (LOW - 1 - k) if f % 2 == 0 else (HIGH + k)
                pads[f // 2][c, row : row + 1, :] = value


def stage_kernel(second_stage, step, *refs):
    refs = list(refs)
    ints, floats = refs[0:2]
    state, state_t, bed, bed_t, rough = refs[2:7]
    at = 7
    base = None
    if second_stage:
        base = refs[7]
        at = 8
    own, got = refs[at : at + 4], refs[at + 4 : at + 8]
    at += 8
    last = second_stage and step == STEPS - 1
    out = refs[at]
    at += 1
    if not last:
        out_t, outs = refs[at], refs[at + 1 : at + 5]
        at += 5
    pad_x, pad_y, flux_x, flux_y, div_x = refs[at:]
    patch = pl.program_id(0)
    for c in range(3):
        pad_y[c, LOW:HIGH, :] = state[0, c]
        pad_x[c, LOW:HIGH, :] = state_t[0, c]
    pad_y[3, LOW:HIGH, :] = bed[0]
    pad_x[3, LOW:HIGH, :] = bed_t[0]
    write_ghosts(patch, ints, own, got, (pad_x, pad_y))
    fluxes(pad_x, flux_x, 1, 2)
    for chunk in range(16):
        r = 8 * chunk
        for q, value in enumerate(divergence(pad_x, flux_x, r)):
            div_x[q, r : r + 8, :] = value
    fluxes(pad_y, flux_y, 2, 1)
    for q in range(3):
        flux_x[q, 0:128, :] = div_x[q].T
    dt = floats[step]
    over = dt * floats[STEPS + patch]
    for chunk in range(16):
        r = 8 * chunk
        rows = slice(r, r + 8)
        mass, north, east = divergence(pad_y, flux_y, r)
        h, hu, hv = (state[0, c, rows, :] for c in range(3))
        n = rough[0, rows, :]
        drag = (dt * GRAVITY) * n * n * jnp.sqrt(hu * hu + hv * hv)
        drag = drag * jnp.exp((-7.0 / 3.0) * jnp.log(h))
        new = (
            h - over * (mass + flux_x[0, rows, :]),
            hu - over * (east + flux_x[1, rows, :]) - drag * hu,
            hv - over * (north + flux_x[2, rows, :]) - drag * hv,
        )
        for c in range(3):
            if second_stage:
                out[0, c, rows, :] = 0.5 * base[0, c, rows, :] + 0.5 * new[c]
            else:
                out[0, c, rows, :] = new[c]
    if not last:
        for c in range(3):
            out_t[0, c] = out[0, c].T
        write_strips(
            lambda c, d: out[0, c, d : d + 1, :] if c < 3 else bed[0, d : d + 1, :],
            lambda c, d: out_t[0, c, d : d + 1, :] if c < 3 else bed_t[0, d : d + 1, :],
            outs,
        )


def patch_spec(*shape):
    return pl.BlockSpec((1,) + shape, lambda i: (i,) + (0,) * len(shape))


def stage(second_stage, step, ints, floats, state, state_t, bed, bed_t, rough, base, own, got):
    owned = bed.shape[0]
    whole = pl.BlockSpec((owned, 16, 128), lambda i: (0, 0, 0))
    smem = pl.BlockSpec(memory_space=pltpu.SMEM)
    full, flat, strip = patch_spec(3, 128, 128), patch_spec(128, 128), patch_spec(16, 128)
    in_specs = [smem, smem, full, full, flat, flat, flat]
    args = [ints, floats, state, state_t, bed, bed_t, rough]
    if second_stage:
        in_specs.append(full)
        args.append(base)
    in_specs += [whole] * 8
    args += list(own) + list(got)
    field = jax.ShapeDtypeStruct(state.shape, jnp.float32)
    out_shape, out_specs = [field], [full]
    if not (second_stage and step == STEPS - 1):
        out_shape += [field] + [jax.ShapeDtypeStruct((owned, 16, 128), jnp.float32)] * 4
        out_specs += [full] + [strip] * 4
    scratch = [
        pltpu.VMEM((4, 152, 128), jnp.float32),
        pltpu.VMEM((4, 152, 128), jnp.float32),
        pltpu.VMEM((3, 136, 128), jnp.float32),
        pltpu.VMEM((3, 136, 128), jnp.float32),
        pltpu.VMEM((3, 128, 128), jnp.float32),
    ]
    got_out = pl.pallas_call(
        functools.partial(stage_kernel, second_stage, step),
        grid=(owned,),
        in_specs=in_specs,
        out_specs=out_specs,
        out_shape=out_shape,
        scratch_shapes=scratch,
        name="stage",
    )(*args)
    if len(got_out) == 1:
        return got_out[0], None, None
    return got_out[0], got_out[1], got_out[2:]


def sends_of(axis):
    index, devices = lax.axis_index(axis), lax.axis_size(axis)
    up = ({axis: lax.rem(index + 1, devices)}, index < devices - 1, index > 0)
    down = ({axis: lax.rem(index + devices - 1, devices)}, index > 0, index < devices - 1)
    return up, down


def greet(links):
    barrier = pltpu.get_barrier_semaphore()
    for target, sends, _ in links:

        @pl.when(sends)
        def _(target=target):
            pl.semaphore_signal(
                barrier, inc=1, device_id=target, device_id_type=pl.DeviceIdType.MESH
            )

    pl.semaphore_wait(barrier, sum(sends.astype(jnp.int32) for _, sends, _ in links))


def remote(source, target, send_sem, recv_sem, link):
    return pltpu.make_async_remote_copy(
        src_ref=source,
        dst_ref=target,
        send_sem=send_sem,
        recv_sem=recv_sem,
        device_id=link[0],
        device_id_type=pl.DeviceIdType.MESH,
    )


def finish(copies):
    for copy, link in copies:
        pl.when(link[2])(copy.wait_recv)
    for copy, link in copies:
        pl.when(link[1])(copy.wait_send)


def exchange_kernel(west, east, south, north, *refs):
    got, send_sem, recv_sem = refs[:4], refs[4], refs[5]
    links = sends_of("gx") + sends_of("gy")
    greet(links)
    copies = []
    for d, source in enumerate((east, west, north, south)):
        copy = remote(source, got[d], send_sem.at[d], recv_sem.at[d], links[d])
        pl.when(links[d][1])(copy.start)
        copies.append((copy, links[d]))
    finish(copies)


def exchange(strips):
    anywhere = pl.BlockSpec(memory_space=pl.ANY)
    return pl.pallas_call(
        exchange_kernel,
        in_specs=[anywhere] * 4,
        out_specs=[anywhere] * 4,
        out_shape=[jax.ShapeDtypeStruct(strips[0].shape, jnp.float32)] * 4,
        scratch_shapes=[pltpu.SemaphoreType.DMA((4,)), pltpu.SemaphoreType.DMA((4,))],
        compiler_params=pltpu.CompilerParams(collective_id=0, has_side_effects=True),
        name="exchange",
    )(*strips)


PIECE = 2


def rebalance_kernel(indices, table, low, high, packed, send_sem, recv_sem):
    links = sends_of("gx")
    greet(links)
    copies = []
    for piece in range(MOVE // PIECE):
        for d, target in enumerate((low, high)):
            begin = piece * PIECE
            for k in range(PIECE):
                packed[d * MOVE + begin + k] = table[indices[d * MOVE + begin + k]]
            n = d * (MOVE // PIECE) + piece
            copy = remote(
                packed.at[pl.ds(d * MOVE + begin, PIECE)],
                target.at[pl.ds(begin, PIECE)],
                send_sem.at[n],
                recv_sem.at[n],
                links[d],
            )
            pl.when(links[d][1])(copy.start)
            copies.append((copy, links[d]))
    finish(copies)


def rebalance(table, indices):
    anywhere = pl.BlockSpec(memory_space=pl.ANY)
    pieces = 2 * (MOVE // PIECE)
    patch = table.shape[1:]
    return pl.pallas_call(
        rebalance_kernel,
        in_specs=[pl.BlockSpec(memory_space=pltpu.SMEM), pl.BlockSpec(memory_space=pltpu.VMEM)],
        out_specs=[anywhere] * 2,
        out_shape=[jax.ShapeDtypeStruct((MOVE,) + patch, jnp.float32)] * 2,
        scratch_shapes=[
            pltpu.VMEM((2 * MOVE,) + patch, jnp.float32),
            pltpu.SemaphoreType.DMA((pieces,)),
            pltpu.SemaphoreType.DMA((pieces,)),
        ],
        compiler_params=pltpu.CompilerParams(collective_id=1, has_side_effects=True),
        name="rebalance",
    )(indices, table)


def assemble(picks, old_state, from_low, from_high, bed):
    owned = bed.shape[0]

    def body(picks_ref, here, low, high, bed_ref, state, state_t, bed_t, *strips):
        where = picks_ref[0, pl.program_id(0)]
        for c in range(3):
            value = jnp.where(where == 0, low[0, c], jnp.where(where == 2, high[0, c], here[0, c]))
            state[0, c] = value
            state_t[0, c] = value.T
        bed_t[0] = bed_ref[0].T
        write_strips(
            lambda c, d: state[0, c, d : d + 1, :] if c < 3 else bed_ref[0, d : d + 1, :],
            lambda c, d: state_t[0, c, d : d + 1, :] if c < 3 else bed_t[0, d : d + 1, :],
            strips,
        )

    def chosen(row):
        return pl.BlockSpec((1, 3, 128, 128), lambda i, ind: (ind[row, i], 0, 0, 0))

    def each(*shape):
        return pl.BlockSpec((1,) + shape, lambda i, ind: (i,) + (0,) * len(shape))

    field = jax.ShapeDtypeStruct((owned, 3, 128, 128), jnp.float32)
    strip = jax.ShapeDtypeStruct((owned, 16, 128), jnp.float32)
    out = pl.pallas_call(
        body,
        grid_spec=pltpu.PrefetchScalarGridSpec(
            num_scalar_prefetch=1,
            grid=(owned,),
            in_specs=[chosen(1), chosen(2), chosen(3), each(128, 128)],
            out_specs=[each(3, 128, 128), each(3, 128, 128), each(128, 128)] + [each(16, 128)] * 4,
        ),
        out_shape=[field, field, jax.ShapeDtypeStruct(bed.shape, jnp.float32)] + [strip] * 4,
        name="assemble",
    )(picks, old_state, from_low, from_high, bed)
    return out[0], out[1], out[2], out[3:]


def on_device(old_state, bed, roughness, levels, sources, neighbours, face_codes, step_index):
    owned = levels.shape[0]
    capacity = old_state.shape[0]
    across = lax.axis_size("gy")
    device = lax.axis_index("gx") * across + lax.axis_index("gy")
    slots = jnp.arange(MOVE, dtype=jnp.int32)

    def listed(target):
        return lax.dynamic_slice_in_dim(sources, target * owned, owned)

    mine = listed(device)
    lists = jnp.stack([listed(device + across), listed(device - across), mine, mine])
    holders = jnp.stack([device, device, device - across, device + across])
    masks = lists // capacity == holders[:, None]
    count = jnp.arange(owned)
    before = (count[:, None] > count[None, :])[None]
    ranks = jnp.sum(jnp.where(before & masks[:, None, :], 1, 0), axis=2)
    hits = masks[:2, None, :] & (ranks[:2, None, :] == slots[None, :, None])
    sends = jnp.sum(jnp.where(hits, lists[:2, None, :] % capacity, 0), axis=2).reshape(-1)
    from_low, from_high = rebalance(old_state, sends.astype(jnp.int32))

    is_low, is_high = masks[2], masks[3]
    picks = jnp.stack(
        [
            jnp.where(is_low, 0, jnp.where(is_high, 2, 1)),
            jnp.where(is_low | is_high, 0, mine % capacity),
            jnp.where(is_low, jnp.minimum(ranks[2], MOVE - 1), 0),
            jnp.where(is_high, jnp.minimum(ranks[3], MOVE - 1), 0),
        ]
    ).astype(jnp.int32)
    state, state_t, bed_t, strips = assemble(picks, old_state, from_low, from_high, bed)

    named = jnp.maximum(neighbours, 0)
    far = jnp.where(named // owned != device, 1, 0)
    ints = jnp.concatenate([named % owned, far, face_codes], axis=1).astype(jnp.int32)
    spacing = jnp.where(
        levels == 0, COARSE_SPACING, jnp.where(levels == 1, COARSE_SPACING / 2, COARSE_SPACING / 4)
    ).astype(jnp.float32)
    step_sizes = STEP_BASE * (2.0 + step_index.astype(jnp.float32)) / 5.0
    floats = jnp.concatenate([step_sizes, 1.0 / spacing])

    for step in range(STEPS):
        base = state
        got = exchange(strips)
        section, section_t, strips = stage(
            False, step, ints, floats, state, state_t, bed, bed_t, roughness, None, strips, got
        )
        got = exchange(strips)
        state, state_t, strips = stage(
            True, step, ints, floats, section, section_t, bed, bed_t, roughness, base, strips, got
        )
    return state


def solution(mesh):
    in_specs = (
        P(("env", "gx", "gy"), None, None, None),
        P(("env", "gx", "gy"), None, None),
        P(("env", "gx", "gy"), None, None),
        P(("env", "gx", "gy")),
        P("env"),
        P(("env", "gx", "gy"), None),
        P(("env", "gx", "gy"), None),
        P("env"),
    )
    out_specs = P(("env", "gx", "gy"), None, None, None)
    return jax.shard_map(
        on_device, mesh=mesh, in_specs=in_specs, out_specs=out_specs, check_vma=False
    )
```
